32 devices in a mesh: obs: 16 (over z, y, x), chan: 2 (over core).
Axes of the slice: x: 2, y: 2, z: 4, core: 2. Of those that a mesh axis runs over, the one named last changes fastest.
Arguments:
- observed: bfloat16 [16384, 128], P('obs', 'chan'), may hold values from -6 to 6
- predictors: bfloat16 [16384, 128], P('obs'), may hold values from -6 to 6
- cells: int32 [16384], P('obs'), may hold values from 0 to 65535, as said below
- columns: bfloat16 [65536, 274], P('obs'), may hold values from -6 to 6
- obs_error: float32 [128], P('chan'), may hold values from 0.5 to 2
- w_col: bfloat16 [274, 1024], P(None, 'chan'), may hold values from -0.3125 to 0.3125
- w_pred: bfloat16 [128, 1024], P(None, 'chan'), may hold values from -0.3125 to 0.3125
- w_mid: bfloat16 [1024, 1024], P(None, 'chan'), may hold values from -0.1875 to 0.1875
- w_out: bfloat16 [1024, 128], P('chan'), may hold values from -0.375 to 0.375
Outputs:
- departures: float32 [16384, 128], P('obs', 'chan')
The draws below stay inside these ranges and needn't reach their ends.
Inputs may be any that keep to these rules, and one draw needn't show every extreme that they name: `cells`: the owner of cell c is c // 4096. Among the 1024 footprints of one index of obs, at most 160 fall on any one owner; in every draw 1 owners receive exactly 160 from every index of obs.
All inputs are finite; a program needn't handle non-finite values.
Results may differ from the reference program's by a relative error of at most 0.0028.
Values may be sent and summed in bfloat16 or wider, within the bound.
A program may use at most 64 MiB of HBM per device.

```python
import math
import jax
import jax.numpy as jnp
from jax import lax

PRED = 128
HID = 1024
CHAN = 128
FOOT_DEV = 1024
CELL_DEV = 4096
CF = 274
SHARDS = 16
CAP = 160
HOT = 1
FOOT = 16384
CELLS = 65536


def draw_cells(key, part):
    slots = SHARDS * CAP
    hot_owner = jax.random.permutation(jax.random.fold_in(key, 1), SHARDS) < HOT

    def one_block(block):
        block_key = jax.random.fold_in(key, 100 + block)
        owner_of_slot = jnp.arange(slots, dtype=jnp.int32) // CAP
        order = jax.random.permutation(jax.random.fold_in(block_key, 1), slots).astype(jnp.int32)
        priority = jnp.where(hot_owner[owner_of_slot], 0, slots).astype(jnp.int32) + order
        chosen = jnp.argsort(priority)[:FOOT_DEV].astype(jnp.int32)
        chosen = jax.random.permutation(jax.random.fold_in(block_key, 2), chosen)
        owner = chosen // CAP
        within = jax.random.randint(jax.random.fold_in(block_key, 3), (FOOT_DEV,), 0, CELL_DEV, dtype=jnp.int32)
        return (owner * CELL_DEV + within).astype(jnp.int32)
    return lax.map(one_block, jnp.arange(SHARDS, dtype=jnp.int32)).reshape(-1)


def steps_of(own_key, extent, split, smallest, largest):
    gain = 1.0
    for position, shards_of in split:
        draws = jax.random.uniform(jax.random.fold_in(jax.random.fold_in(own_key, 6), position), (shards_of,), jnp.float32, smallest / len(split), largest / len(split))
        gain = gain * jnp.repeat(jnp.exp(draws), extent[position] // shards_of).reshape((-1,) + (1,) * (len(extent) - 1 - position))
    return gain


def normal_values(key, shape, deviation, bound, cuts=(), kind=jnp.bfloat16):
    factor_of = steps_of(key, shape, cuts, -0.22, 0.18) if cuts else 1.0
    values = jax.random.normal(key, shape, jnp.float32) * deviation * factor_of
    return jnp.minimum(jnp.maximum(values, -bound), bound).astype(kind)


def setup_inputs(seed: int = 0) -> dict:
    keys = jax.random.split(jax.random.key(seed), 10)
    observed = normal_values(keys[0], (FOOT, CHAN), 1.0, 6.0, ((0, 16), (1, 2)))
    predictors = normal_values(keys[1], (FOOT, PRED), 1.0, 6.0, ((0, 16),))
    cells = draw_cells(jax.random.fold_in(keys[9], 71), 0)
    columns = normal_values(keys[3], (CELLS, CF), 1.0, 6.0, ((0, 16),))
    obs_error = jnp.clip(jnp.exp(math.log(2.0) - 1.3862944 * jax.random.uniform(keys[4], (CHAN,), jnp.float32) ** steps_of(keys[4], (CHAN,), ((0, 2),), -0.2, 0.2)), 0.5, 2.0)
    w_col = normal_values(keys[5], (CF, HID), (CF + PRED) ** -0.5, 0.3125, ((1, 2),))
    w_pred = normal_values(keys[6], (PRED, HID), (CF + PRED) ** -0.5, 0.3125, ((1, 2),))
    w_mid = normal_values(keys[7], (HID, HID), HID ** -0.5, 0.1875, ((1, 2),))
    w_out = normal_values(keys[8], (HID, CHAN), (HID // 4) ** -0.5, 0.375, ((0, 2),))
    return {"observed": observed, "predictors": predictors, "cells": cells, "columns": columns, "obs_error": obs_error, "w_col": w_col, "w_pred": w_pred, "w_mid": w_mid, "w_out": w_out}


def reference(observed, predictors, cells, columns, obs_error, w_col, w_pred, w_mid, w_out):
    total = cells.shape[0]
    block = math.gcd(total, 4096)

    def evolve(pieces):
        cell_block, pred_block = pieces
        column = jnp.take(columns, cell_block, axis=0)
        first = jnp.dot(column, w_col, preferred_element_type=jnp.float32)
        first = first + jnp.dot(pred_block, w_pred, preferred_element_type=jnp.float32)
        hidden = jax.nn.silu(first).astype(jnp.bfloat16)
        upper = jax.nn.silu(jnp.dot(hidden, w_mid, preferred_element_type=jnp.float32)).astype(jnp.bfloat16)
        return jnp.dot(upper, w_out, preferred_element_type=jnp.float32)

    evolved = lax.map(evolve, (cells.reshape(total // block, block), predictors.reshape(total // block, block, predictors.shape[1])))
    evolved = evolved.reshape(total, w_out.shape[1])
    return (observed.astype(jnp.float32) - evolved) / obs_error[None, :]
```

```python
import functools

import jax
import jax.numpy as jnp
from jax import lax
from jax.experimental import pallas as pl
from jax.experimental.pallas import tpu as pltpu
from jax.sharding import PartitionSpec as P

MESH = pl.DeviceIdType.MESH
LANES = 128
PACK = 24
F32 = jnp.float32
BF16 = jnp.bfloat16


def silu(v):
    h = v * 0.5
    return (h + h * jnp.tanh(h)).astype(BF16)


def dot(a, b):
    return jnp.dot(a, b, preferred_element_type=F32)


def kernel(
    n, slots,
    cells, pred, observed, err, columns, wc, wp, wm, wo,
    out,
    cellv, colv, tab, stage, idx_send, idx_recv, idx_s, sendbuf, recv, tcol, acc,
    predv, obsv, errv, wc_own, wc_oth, wp_own, wp_oth, wm_own, wm_oth, wo_own, wo_oth,
    rem32, w2_own, w2_oth, ev_send, ev_recv,
    in_sem, idx_ssem, idx_rsem, col_ssem, col_rsem, fwd_ssem, fwd_rsem, w_ssem, w_rsem,
    ev_ssem, ev_rsem, smem_sem,
):
    me = lax.axis_index("obs")
    core = lax.axis_index("chan")
    other = 1 - core
    count = cells.shape[1]
    half = count // 2
    cf, cell_dev = columns.shape
    main = 2 * LANES
    extra = cf - main
    groups = slots // 16

    loads = [
        pltpu.make_async_copy(src, dst, in_sem.at[i])
        for i, (src, dst) in enumerate(
            [
                (cells, cellv),
                (columns, colv),
                (pred.at[pl.ds(core * half, half)], predv),
                (observed, obsv),
                (err, errv),
                (wc, wc_own),
                (wp, wp_own),
                (wm, wm_own),
                (wo, wo_own),
            ]
        )
    ]
    for load in loads:
        load.start()

    barrier = pltpu.get_barrier_semaphore()

    @pl.loop(1, n)
    def _(t):
        pl.semaphore_signal(
            barrier, inc=1, device_id=(lax.rem(me + t, n), core), device_id_type=MESH
        )

    pl.semaphore_signal(barrier, inc=1, device_id=(me, other), device_id_type=MESH)

    loads[0].wait()
    cell = cellv[...]
    owner = cell >> (cell_dev.bit_length() - 1)
    local = cell & (cell_dev - 1)
    hot = (owner == lax.broadcasted_iota(jnp.int32, (n, count), 0)).astype(F32)
    blocks = count // LANES
    cut = [hot[:, b * LANES : (b + 1) * LANES] for b in range(blocks)]
    upto = (
        lax.broadcasted_iota(jnp.int32, (LANES, LANES), 0)
        <= lax.broadcasted_iota(jnp.int32, (LANES, LANES), 1)
    )
    upto = upto.astype(F32).astype(BF16)
    inside = dot(jnp.concatenate(cut, axis=0).astype(BF16), upto)
    run = jnp.zeros((n, 1), F32)
    ranks = []
    for b in range(blocks):
        part = inside[b * n : (b + 1) * n]
        before = part - cut[b] + run
        ranks.append(jnp.sum(before * cut[b], axis=0, keepdims=True))
        run = run + part[:, LANES - 1 : LANES]
    rank = jnp.concatenate(ranks, axis=1).astype(jnp.int32)
    side = rank & 1
    place = rank >> 1
    mine = hot * (side == core).astype(F32)
    high = (local >> 6).astype(F32)
    low = (local & 63).astype(F32)
    values = jnp.concatenate([mine * high, mine * low], axis=0).astype(BF16)
    at = (place == lax.broadcasted_iota(jnp.int32, (LANES, count), 0)).astype(F32).astype(BF16)
    asked = lax.dot_general(values, at, (((1,), (1,)), ((), ())), preferred_element_type=F32)
    asked = (asked[:n] * 64.0 + asked[n:]).astype(jnp.int32) & (cell_dev - 1)
    for o in range(n):
        idx_send[o] = asked[o : o + 1]

    pl.semaphore_wait(barrier, n)

    def idx_copy(t):
        return pltpu.make_async_remote_copy(
            src_ref=idx_send.at[lax.rem(me + t, n)],
            dst_ref=idx_recv.at[me],
            send_sem=idx_ssem.at[t],
            recv_sem=idx_rsem.at[t],
            device_id=(lax.rem(me + t, n), core),
            device_id_type=MESH,
        )

    @pl.loop(1, n)
    def _(t):
        idx_copy(t).start()

    swaps = [
        pltpu.make_async_remote_copy(
            src_ref=src, dst_ref=dst, send_sem=w_ssem.at[i], recv_sem=w_rsem.at[i],
            device_id=(me, other), device_id_type=MESH,
        )
        for i, (src, dst) in enumerate([(wc, wc_oth), (wp, wp_oth), (wm, wm_oth), (wo, wo_oth)])
    ]
    for swap in swaps:
        swap.start()

    idx_recv[me] = idx_send[me]
    target = (owner * (2 * slots) + side * slots + place).astype(F32)
    target = jnp.where(core == 0, target[:, :half], target[:, half:])
    tcol[...] = jnp.transpose(jnp.broadcast_to(target, (LANES, half))).astype(jnp.int32)
    acc[...] = jnp.zeros_like(acc)

    loads[1].wait()
    rows = 256
    unit = (
        lax.broadcasted_iota(jnp.int32, (rows, rows), 0)
        == lax.broadcasted_iota(jnp.int32, (rows, rows), 1)
    )
    unit = unit.astype(F32).astype(BF16)

    def turn(x):
        return lax.dot_general(unit, x, (((1,), (1,)), ((), ())), preferred_element_type=F32)

    @pl.loop(0, cell_dev // rows)
    def _(i):
        at_rows = pl.ds(pl.multiple_of(i * rows, rows), rows)
        tab[at_rows, 0:main] = turn(colv[0:main, at_rows])
        tab[at_rows, main : main + LANES] = jnp.zeros((rows, LANES), F32)
        tab[at_rows, main:cf] = turn(colv[main:cf, at_rows])

    @pl.loop(1, n)
    def _(t):
        idx_copy(t).wait_recv()

    to_smem = pltpu.make_async_copy(idx_recv, idx_s, smem_sem)
    to_smem.start()
    to_smem.wait()

    def gather(asker, dst):
        for k in range(slots):
            stage[k : k + 1, :] = tab[pl.ds(idx_s[asker, 0, k] & (cell_dev - 1), 1), :]
        dst[0:slots, :] = stage[:, 0:LANES].astype(BF16)
        dst[slots : 2 * slots, :] = stage[:, LANES:main].astype(BF16)
        packed = stage[0:16, main:]
        for j in range(1, groups):
            packed = packed + pltpu.roll(stage[16 * j : 16 * j + 16, main:], PACK * j, 1)
        dst[2 * slots : 2 * slots + 16, :] = packed.astype(BF16)

    def col_copy(t):
        asker = lax.rem(me + t, n)
        return pltpu.make_async_remote_copy(
            src_ref=sendbuf.at[asker],
            dst_ref=recv.at[core, me],
            send_sem=col_ssem.at[t],
            recv_sem=col_rsem.at[t],
            device_id=(asker, core),
            device_id_type=MESH,
        )

    def forward(t):
        o = lax.rem(me + n - t, n)
        return pltpu.make_async_remote_copy(
            src_ref=recv.at[core, o],
            dst_ref=recv.at[core, o],
            send_sem=fwd_ssem.at[t],
            recv_sem=fwd_rsem.at[t],
            device_id=(me, other),
            device_id_type=MESH,
        )

    @pl.loop(1, n)
    def _(t):
        asker = lax.rem(me + t, n)
        gather(asker, sendbuf.at[asker])
        col_copy(t).start()

    gather(me, recv.at[core, me])
    forward(0).start()

    for load in loads[2:]:
        load.wait()
    rem32[...] = jnp.zeros_like(rem32)

    def tail(wc_ref, wp_ref, w2):
        rem32[0:extra, :] = wc_ref[main:cf, :].astype(F32)
        w2[0:LANES, :] = rem32[...].astype(BF16)
        w2[LANES:, :] = wp_ref[...]

    tail(wc_own, wp_own, w2_own)
    for swap in swaps:
        swap.wait()
    tail(wc_oth, wp_oth, w2_oth)

    def place_rows(t):
        o = lax.rem(me + n - t, n)
        forward(t).wait_recv()
        sides = []
        for s in range(2):
            packed = recv[s, o, 2 * slots : 2 * slots + 16, :].astype(F32)
            rest = [packed] + [pltpu.roll(packed, LANES - PACK * j, 1) for j in range(1, groups)]
            sides.append(
                jnp.concatenate(
                    [
                        recv[s, o, 0:slots, :],
                        recv[s, o, slots : 2 * slots, :],
                        jnp.concatenate(rest, axis=0).astype(BF16),
                    ],
                    axis=1,
                )
            )
        data = jnp.concatenate(sides, axis=0)
        want = tcol[...] - o * (2 * slots)
        lane = lax.broadcasted_iota(jnp.int32, (half, LANES), 1)
        pick = [
            (want == lane + b).astype(F32).astype(BF16)[:, : min(LANES, 2 * slots - b)]
            for b in range(0, 2 * slots, LANES)
        ]
        acc[...] += dot(jnp.concatenate(pick, axis=1), data)

    @pl.loop(1, n)
    def _(t):
        col_copy(t).wait_recv()
        forward(t).start()
        place_rows(t - 1)

    place_rows(n - 1)

    parts = 2
    chunk = half // parts
    here = pl.ds(pl.multiple_of(core * wc.shape[1], wc.shape[1]), wc.shape[1])
    there = pl.ds(pl.multiple_of(other * wc.shape[1], wc.shape[1]), wc.shape[1])
    chan = out.shape[0]
    spread = jnp.broadcast_to(errv[...], (chan, chan))
    diagonal = (
        lax.broadcasted_iota(jnp.int32, (chan, chan), 0)
        == lax.broadcasted_iota(jnp.int32, (chan, chan), 1)
    )
    error = jnp.sum(jnp.where(diagonal, spread, 0.0), axis=1, keepdims=True)

    def ev_copy(p):
        return pltpu.make_async_remote_copy(
            src_ref=ev_send.at[p], dst_ref=ev_recv.at[p],
            send_sem=ev_ssem.at[p], recv_sem=ev_rsem.at[p],
            device_id=(me, other), device_id_type=MESH,
        )

    for p in range(parts):
        rows_p = slice(p * chunk, (p + 1) * chunk)
        a = acc[rows_p, 0:main].astype(BF16)
        b = jnp.concatenate([acc[rows_p, main:].astype(BF16), predv[rows_p, :]], axis=1)
        h_own = silu(dot(a, wc_own[0:main, :]) + dot(b, w2_own[...]))
        h_oth = silu(dot(a, wc_oth[0:main, :]) + dot(b, w2_oth[...]))
        u_own = silu(dot(h_own, wm_own[here, :]) + dot(h_oth, wm_own[there, :]))
        u_oth = silu(dot(h_own, wm_oth[here, :]) + dot(h_oth, wm_oth[there, :]))
        e = jnp.transpose(dot(u_own, wo_own[...]) + dot(u_oth, wo_oth[...]))
        ev_send[p] = jnp.where(core == 0, e[chan:], e[:chan])
        ev_copy(p).start()
        keep = jnp.where(core == 0, e[:chan], e[chan:])
        at_rows = pl.ds(pl.multiple_of(core * half + p * chunk, chunk), chunk)
        out[:, at_rows] = (obsv[:, at_rows].astype(F32) - keep) / error

    for p in range(parts):
        ev_copy(p).wait_recv()
        at_rows = pl.ds(pl.multiple_of(other * half + p * chunk, chunk), chunk)
        out[:, at_rows] = (obsv[:, at_rows].astype(F32) - ev_recv[p]) / error

    for p in range(parts):
        ev_copy(p).wait_send()
    forward(0).wait_send()

    @pl.loop(1, n)
    def _(t):
        idx_copy(t).wait_send()
        col_copy(t).wait_send()
        forward(t).wait_send()


def on_device(observed, predictors, cells, columns, obs_error, w_col, w_pred, w_mid, w_out):
    n = lax.axis_size("obs")
    count = cells.shape[0]
    cell_dev, cf = columns.shape
    cap = 5 * count // (2 * n)
    slots = (-(-cap // 2) + 15) // 16 * 16
    half = count // 2
    chan = observed.shape[1]
    hid = w_col.shape[1]
    packet = 2 * slots + 16
    dma = pltpu.SemaphoreType.DMA
    vmem = pltpu.VMEM
    any_ = pl.BlockSpec(memory_space=pl.ANY)
    return pl.pallas_call(
        functools.partial(kernel, n, slots),
        out_shape=jax.ShapeDtypeStruct((chan, count), F32),
        in_specs=[any_] * 9,
        out_specs=pl.BlockSpec(memory_space=pltpu.VMEM),
        scratch_shapes=[
            vmem((1, count), jnp.int32),
            vmem((cf, cell_dev), BF16),
            vmem((cell_dev, 3 * LANES), F32),
            vmem((slots, 3 * LANES), F32),
            vmem((n, 1, LANES), jnp.int32),
            vmem((n, 1, LANES), jnp.int32),
            pltpu.SMEM((n, 1, LANES), jnp.int32),
            vmem((n, packet, LANES), BF16),
            vmem((2, n, packet, LANES), BF16),
            vmem((half, LANES), jnp.int32),
            vmem((half, 3 * LANES), F32),
            vmem((half, predictors.shape[1]), BF16),
            vmem((chan, count), BF16),
            vmem((1, chan), F32),
            vmem(w_col.shape, BF16),
            vmem(w_col.shape, BF16),
            vmem(w_pred.shape, BF16),
            vmem(w_pred.shape, BF16),
            vmem(w_mid.shape, BF16),
            vmem(w_mid.shape, BF16),
            vmem(w_out.shape, BF16),
            vmem(w_out.shape, BF16),
            vmem((LANES, hid), F32),
            vmem((LANES + w_pred.shape[0], hid), BF16),
            vmem((LANES + w_pred.shape[0], hid), BF16),
            vmem((2, chan, half // 2), F32),
            vmem((2, chan, half // 2), F32),
            dma((9,)),
            dma((n,)), dma((n,)), dma((n,)), dma((n,)), dma((n,)), dma((n,)),
            dma((4,)), dma((4,)),
            dma((2,)), dma((2,)),
            dma,
        ],
        compiler_params=pltpu.CompilerParams(
            collective_id=0, has_side_effects=True, vmem_limit_bytes=60 * 1024 * 1024
        ),
    )(
        cells.reshape(1, count), predictors, observed.T, obs_error.reshape(1, chan), columns.T,
        w_col, w_pred, w_mid, w_out,
    ).T


def solution(mesh):
    return jax.shard_map(
        on_device,
        mesh=mesh,
        in_specs=(
            P("obs", "chan"),
            P("obs", None),
            P("obs"),
            P("obs", None),
            P("chan"),
            P(None, "chan"),
            P(None, "chan"),
            P(None, "chan"),
            P("chan", None),
        ),
        out_specs=P("obs", "chan"),
        check_vma=False,
    )
```

```python
import functools

import jax
import jax.numpy as jnp
from jax import lax
from jax.experimental import pallas as pl
from jax.experimental.pallas import tpu as pltpu
from jax.sharding import PartitionSpec as P

MESH = pl.DeviceIdType.MESH
LANES = 128
PACK = 24
F32 = jnp.float32
BF16 = jnp.bfloat16


def silu(v):
    h = v * 0.5
    return (h + h * jnp.tanh(h)).astype(BF16)


def dot(a, b):
    return jnp.dot(a, b, preferred_element_type=F32)


def kernel(
    n, slots,
    cells, pred, observed, err, columns, wc, wp, wm, wo,
    out,
    cellv, colv, tab, stage, idx_send, idx_recv, idx_s, sendbuf, recv, tcol, acc,
    predv, obsv, errv, wc_own, wc_oth, wp_own, wp_oth, wm_own, wm_oth, wo_own, wo_oth,
    rem32, w2_own, w2_oth, ev_send, ev_recv,
    in_sem, idx_ssem, idx_rsem, col_ssem, col_rsem, fwd_ssem, fwd_rsem, w_ssem, w_rsem,
    ev_ssem, ev_rsem, smem_sem,
):
    me = lax.axis_index("obs")
    core = lax.axis_index("chan")
    other = 1 - core
    count = cells.shape[1]
    half = count // 2
    cf, cell_dev = columns.shape
    main = 2 * LANES
    extra = cf - main
    groups = slots // 16

    loads = [
        pltpu.make_async_copy(src, dst, in_sem.at[i])
        for i, (src, dst) in enumerate(
            [
                (cells, cellv),
                (columns, colv),
                (pred.at[pl.ds(core * half, half)], predv),
                (observed, obsv),
                (err, errv),
                (wc, wc_own),
                (wp, wp_own),
                (wm, wm_own),
                (wo, wo_own),
            ]
        )
    ]
    for load in loads:
        load.start()

    barrier = pltpu.get_barrier_semaphore()

    @pl.loop(1, n)
    def _(t):
        pl.semaphore_signal(
            barrier, inc=1, device_id=(lax.rem(me + t, n), core), device_id_type=MESH
        )

    pl.semaphore_signal(barrier, inc=1, device_id=(me, other), device_id_type=MESH)

    loads[0].wait()
    cell = cellv[...]
    owner = cell >> (cell_dev.bit_length() - 1)
    local = cell & (cell_dev - 1)
    hot = (owner == lax.broadcasted_iota(jnp.int32, (n, count), 0)).astype(F32)
    blocks = count // LANES
    cut = [hot[:, b * LANES : (b + 1) * LANES] for b in range(blocks)]
    upto = (
        lax.broadcasted_iota(jnp.int32, (LANES, LANES), 0)
        <= lax.broadcasted_iota(jnp.int32, (LANES, LANES), 1)
    )
    upto = upto.astype(F32).astype(BF16)
    inside = dot(jnp.concatenate(cut, axis=0).astype(BF16), upto)
    run = jnp.zeros((n, 1), F32)
    ranks = []
    for b in range(blocks):
        part = inside[b * n : (b + 1) * n]
        before = part - cut[b] + run
        ranks.append(jnp.sum(before * cut[b], axis=0, keepdims=True))
        run = run + part[:, LANES - 1 : LANES]
    rank = jnp.concatenate(ranks, axis=1).astype(jnp.int32)
    side = rank & 1
    place = rank >> 1
    mine = hot * (side == core).astype(F32)
    high = (local >> 6).astype(F32)
    low = (local & 63).astype(F32)
    values = jnp.concatenate([mine * high, mine * low], axis=0).astype(BF16)
    at = (place == lax.broadcasted_iota(jnp.int32, (LANES, count), 0)).astype(F32).astype(BF16)
    asked = lax.dot_general(values, at, (((1,), (1,)), ((), ())), preferred_element_type=F32)
    asked = (asked[:n] * 64.0 + asked[n:]).astype(jnp.int32) & (cell_dev - 1)
    for o in range(n):
        idx_send[o] = asked[o : o + 1]

    pl.semaphore_wait(barrier, n)

    def idx_copy(t):
        return pltpu.make_async_remote_copy(
            src_ref=idx_send.at[lax.rem(me + t, n)],
            dst_ref=idx_recv.at[me],
            send_sem=idx_ssem.at[t],
            recv_sem=idx_rsem.at[t],
            device_id=(lax.rem(me + t, n), core),
            device_id_type=MESH,
        )

    @pl.loop(1, n)
    def _(t):
        idx_copy(t).start()

    swaps = [
        pltpu.make_async_remote_copy(
            src_ref=src, dst_ref=dst, send_sem=w_ssem.at[i], recv_sem=w_rsem.at[i],
            device_id=(me, other), device_id_type=MESH,
        )
        for i, (src, dst) in enumerate([(wc, wc_oth), (wp, wp_oth), (wm, wm_oth), (wo, wo_oth)])
    ]
    for swap in swaps:
        swap.start()

    idx_recv[me] = idx_send[me]
    target = (owner * (2 * slots) + side * slots + place).astype(F32)
    target = jnp.where(core == 0, target[:, :half], target[:, half:])
    tcol[...] = jnp.transpose(jnp.broadcast_to(target, (LANES, half))).astype(jnp.int32)
    acc[...] = jnp.zeros_like(acc)

    loads[1].wait()
    rows = 256
    unit = (
        lax.broadcasted_iota(jnp.int32, (rows, rows), 0)
        == lax.broadcasted_iota(jnp.int32, (rows, rows), 1)
    )
    unit = unit.astype(F32).astype(BF16)

    def turn(x):
        return lax.dot_general(unit, x, (((1,), (1,)), ((), ())), preferred_element_type=F32)

    @pl.loop(0, cell_dev // rows)
    def _(i):
        at_rows = pl.ds(pl.multiple_of(i * rows, rows), rows)
        tab[at_rows, 0:main] = turn(colv[0:main, at_rows])
        tab[at_rows, main : main + LANES] = jnp.zeros((rows, LANES), F32)
        tab[at_rows, main:cf] = turn(colv[main:cf, at_rows])

    @pl.loop(1, n)
    def _(t):
        idx_copy(t).wait_recv()

    to_smem = pltpu.make_async_copy(idx_recv, idx_s, smem_sem)
    to_smem.start()
    to_smem.wait()

    def gather(asker, dst):
        for k in range(slots):
            stage[k : k + 1, :] = tab[pl.ds(idx_s[asker, 0, k] & (cell_dev - 1), 1), :]
        dst[0:slots, :] = stage[:, 0:LANES].astype(BF16)
        dst[slots : 2 * slots, :] = stage[:, LANES:main].astype(BF16)
        packed = stage[0:16, main:]
        for j in range(1, groups):
            packed = packed + pltpu.roll(stage[16 * j : 16 * j + 16, main:], PACK * j, 1)
        dst[2 * slots : 2 * slots + 16, :] = packed.astype(BF16)

    def col_copy(t):
        asker = lax.rem(me + t, n)
        return pltpu.make_async_remote_copy(
            src_ref=sendbuf.at[asker],
            dst_ref=recv.at[core, me],
            send_sem=col_ssem.at[t],
            recv_sem=col_rsem.at[t],
            device_id=(asker, core),
            device_id_type=MESH,
        )

    def forward(t):
        o = lax.rem(me + n - t, n)
        return pltpu.make_async_remote_copy(
            src_ref=recv.at[core, o],
            dst_ref=recv.at[core, o],
            send_sem=fwd_ssem.at[t],
            recv_sem=fwd_rsem.at[t],
            device_id=(me, other),
            device_id_type=MESH,
        )

    def turn_of(j):
        far = n // 2 + (2 * (j & 1) - 1) * (j >> 1)
        return jnp.where(j == 0, 0, far)

    @pl.loop(1, n)
    def _(j):
        t = turn_of(j)
        asker = lax.rem(me + t, n)
        gather(asker, sendbuf.at[asker])
        col_copy(t).start()

    gather(me, recv.at[core, me])
    forward(0).start()

    for load in loads[2:]:
        load.wait()
    rem32[...] = jnp.zeros_like(rem32)

    def tail(wc_ref, wp_ref, w2):
        rem32[0:extra, :] = wc_ref[main:cf, :].astype(F32)
        w2[0:LANES, :] = rem32[...].astype(BF16)
        w2[LANES:, :] = wp_ref[...]

    tail(wc_own, wp_own, w2_own)
    for swap in swaps:
        swap.wait()
    tail(wc_oth, wp_oth, w2_oth)

    batch = 4

    def place_rows(g):
        sides = []
        slot = lax.broadcasted_iota(jnp.int32, (8, batch * 2 * slots), 1)
        wanted = slot
        for i in range(batch):
            t = turn_of(g * batch + i)
            o = lax.rem(me + n - t, n)
            forward(t).wait_recv()
            wanted = jnp.where(slot >= i * 2 * slots, slot + (o - i) * (2 * slots), wanted)
            for s in range(2):
                packed = recv[s, o, 2 * slots : 2 * slots + 16, :].astype(F32)
                rest = [packed]
                rest += [pltpu.roll(packed, LANES - PACK * j, 1) for j in range(1, groups)]
                sides.append(
                    jnp.concatenate(
                        [
                            recv[s, o, 0:slots, :],
                            recv[s, o, slots : 2 * slots, :],
                            jnp.concatenate(rest, axis=0).astype(BF16),
                        ],
                        axis=1,
                    )
                )
        data = jnp.concatenate(sides, axis=0)
        pick = [
            (tcol[...] == wanted[0:1, b : b + LANES]).astype(F32).astype(BF16)
            for b in range(0, batch * 2 * slots, LANES)
        ]
        acc[...] += dot(jnp.concatenate(pick, axis=1), data)

    def pass_on(j):
        t = turn_of(j)
        col_copy(t).wait_recv()
        forward(t).start()

    for j in range(1, batch):
        pass_on(j)

    @pl.loop(1, n // batch)
    def _(g):
        for i in range(batch):
            pass_on(g * batch + i)
        place_rows(g - 1)

    place_rows(n // batch - 1)

    parts = 2
    chunk = half // parts
    here = pl.ds(pl.multiple_of(core * wc.shape[1], wc.shape[1]), wc.shape[1])
    there = pl.ds(pl.multiple_of(other * wc.shape[1], wc.shape[1]), wc.shape[1])
    chan = out.shape[0]
    spread = jnp.broadcast_to(errv[...], (chan, chan))
    diagonal = (
        lax.broadcasted_iota(jnp.int32, (chan, chan), 0)
        == lax.broadcasted_iota(jnp.int32, (chan, chan), 1)
    )
    error = jnp.sum(jnp.where(diagonal, spread, 0.0), axis=1, keepdims=True)

    def ev_copy(p):
        return pltpu.make_async_remote_copy(
            src_ref=ev_send.at[p], dst_ref=ev_recv.at[p],
            send_sem=ev_ssem.at[p], recv_sem=ev_rsem.at[p],
            device_id=(me, other), device_id_type=MESH,
        )

    for p in range(parts):
        rows_p = slice(p * chunk, (p + 1) * chunk)
        a = acc[rows_p, 0:main].astype(BF16)
        b = jnp.concatenate([acc[rows_p, main:].astype(BF16), predv[rows_p, :]], axis=1)
        h_own = silu(dot(a, wc_own[0:main, :]) + dot(b, w2_own[...]))
        h_oth = silu(dot(a, wc_oth[0:main, :]) + dot(b, w2_oth[...]))
        u_own = silu(dot(h_own, wm_own[here, :]) + dot(h_oth, wm_own[there, :]))
        u_oth = silu(dot(h_own, wm_oth[here, :]) + dot(h_oth, wm_oth[there, :]))
        e = jnp.transpose(dot(u_own, wo_own[...]) + dot(u_oth, wo_oth[...]))
        ev_send[p] = jnp.where(core == 0, e[chan:], e[:chan])
        ev_copy(p).start()
        keep = jnp.where(core == 0, e[:chan], e[chan:])
        at_rows = pl.ds(pl.multiple_of(core * half + p * chunk, chunk), chunk)
        out[:, at_rows] = (obsv[:, at_rows].astype(F32) - keep) / error

    for p in range(parts):
        ev_copy(p).wait_recv()
        at_rows = pl.ds(pl.multiple_of(other * half + p * chunk, chunk), chunk)
        out[:, at_rows] = (obsv[:, at_rows].astype(F32) - ev_recv[p]) / error

    for p in range(parts):
        ev_copy(p).wait_send()
    forward(0).wait_send()

    @pl.loop(1, n)
    def _(t):
        idx_copy(t).wait_send()
        col_copy(t).wait_send()
        forward(t).wait_send()


def on_device(observed, predictors, cells, columns, obs_error, w_col, w_pred, w_mid, w_out):
    n = lax.axis_size("obs")
    count = cells.shape[0]
    cell_dev, cf = columns.shape
    cap = 5 * count // (2 * n)
    slots = (-(-cap // 2) + 15) // 16 * 16
    half = count // 2
    chan = observed.shape[1]
    hid = w_col.shape[1]
    packet = 2 * slots + 16
    dma = pltpu.SemaphoreType.DMA
    vmem = pltpu.VMEM
    any_ = pl.BlockSpec(memory_space=pl.ANY)
    return pl.pallas_call(
        functools.partial(kernel, n, slots),
        out_shape=jax.ShapeDtypeStruct((chan, count), F32),
        in_specs=[any_] * 9,
        out_specs=pl.BlockSpec(memory_space=pltpu.VMEM),
        scratch_shapes=[
            vmem((1, count), jnp.int32),
            vmem((cf, cell_dev), BF16),
            vmem((cell_dev, 3 * LANES), F32),
            vmem((slots, 3 * LANES), F32),
            vmem((n, 1, LANES), jnp.int32),
            vmem((n, 1, LANES), jnp.int32),
            pltpu.SMEM((n, 1, LANES), jnp.int32),
            vmem((n, packet, LANES), BF16),
            vmem((2, n, packet, LANES), BF16),
            vmem((half, LANES), jnp.int32),
            vmem((half, 3 * LANES), F32),
            vmem((half, predictors.shape[1]), BF16),
            vmem((chan, count), BF16),
            vmem((1, chan), F32),
            vmem(w_col.shape, BF16),
            vmem(w_col.shape, BF16),
            vmem(w_pred.shape, BF16),
            vmem(w_pred.shape, BF16),
            vmem(w_mid.shape, BF16),
            vmem(w_mid.shape, BF16),
            vmem(w_out.shape, BF16),
            vmem(w_out.shape, BF16),
            vmem((LANES, hid), F32),
            vmem((LANES + w_pred.shape[0], hid), BF16),
            vmem((LANES + w_pred.shape[0], hid), BF16),
            vmem((2, chan, half // 2), F32),
            vmem((2, chan, half // 2), F32),
            dma((9,)),
            dma((n,)), dma((n,)), dma((n,)), dma((n,)), dma((n,)), dma((n,)),
            dma((4,)), dma((4,)),
            dma((2,)), dma((2,)),
            dma,
        ],
        compiler_params=pltpu.CompilerParams(
            collective_id=0, has_side_effects=True, vmem_limit_bytes=60 * 1024 * 1024
        ),
    )(
        cells.reshape(1, count), predictors, observed.T, obs_error.reshape(1, chan), columns.T,
        w_col, w_pred, w_mid, w_out,
    ).T


def solution(mesh):
    return jax.shard_map(
        on_device,
        mesh=mesh,
        in_specs=(
            P("obs", "chan"),
            P("obs", None),
            P("obs"),
            P("obs", None),
            P("chan"),
            P(None, "chan"),
            P(None, "chan"),
            P(None, "chan"),
            P("chan", None),
        ),
        out_specs=P("obs", "chan"),
        check_vma=False,
    )
```
